512 devices in a mesh: fsdp: 64 (over z, y), img: 8 (over x, core).
Axes of the slice: x: 4, y: 4, z: 16, core: 2. Of those that a mesh axis runs over, the one named last changes fastest.
Arguments:
- tokens: bfloat16 [2048, 8192], P('fsdp', 'img'), may hold values from -6 to 6
- norm_gain: float32 [8192], P('img'), may hold values from 0.5 to 2
- w_query: bfloat16 [8192, 8192], P('img', 'fsdp'), may hold values from -0.0625 to 0.0625
- query_gain: float32 [128], replicated, may hold values from 0.5 to 2
- key_cache: bfloat16 [64, 8192, 1024], P('fsdp', 'img'), may hold values from -96 to 96
- value_cache: bfloat16 [64, 8192, 1024], P('fsdp', 'img'), may hold values from -48 to 48
- block_mask: int32 [2048, 8], P('fsdp'), may hold values from 0 to 1, as said below
- image_counts: int32 [512], P('fsdp'), may hold values from 1 to 2
- image_slot: int32 [512, 2], P('fsdp'), may hold values from 0 to 15, as said below
- attn_gate: float32 [1], replicated, may hold values from 0.8 to 2
- w_out: bfloat16 [8192, 8192], P('img', 'fsdp'), may hold values from -0.0625 to 0.0625
Outputs:
- mixed: bfloat16 [2048, 8192], P('img', 'fsdp')
The draws below stay inside these ranges and needn't reach their ends.
Inputs may be any that keep to these rules, and one draw needn't show every extreme that they name: For k < image_counts[s], image k of sequence s is cached in rows image_slot[s, k] * 512 to (image_slot[s, k] + 1) * 512 - 1 of its group's caches; these entries are distinct within a group. Entries with k >= image_counts[s] name no image. `block_mask`: entry 0 of every row is 1: every text position attends the first key block of its sequence's first image.
All inputs are finite; a program needn't handle non-finite values.
Results may differ from the reference program's by a relative error of at most 0.0085.
The reference program's roundings to bfloat16 on the way count: a program that leaves them out, or rounds other values in their place, can miss the bound.
Values may be sent and summed in bfloat16 or wider, within the bound.
No kernel may reach another device: no remote copies, remote signals or barrier semaphores. Data moves between devices by JAX's collectives and lax.ppermute only.
A program may use at most 64 MiB of HBM per device.

```python
import math
import jax
import jax.numpy as jnp
from jax import lax

D = 8192
H = 64
KVH = 8
HD = 128
IMG_BLK = 4
BLOCK_TOK = 128
SLOTS = 2
MAXIMG = 2
STEPS = 4
HQ = 8192
IMG_TOK = 512
GROUPS = 64
SEQS = 512
TOKENS = 2048
KEYS = 8192


def image_layout(key):
    key = jax.random.fold_in(key, 101)
    count_key, order_key, spare_key = jax.random.split(key, 3)
    per_group = SEQS // GROUPS
    slot_count = KEYS // IMG_TOK
    counts = jax.random.randint(count_key, (GROUPS, per_group), 1, MAXIMG + 1)
    counts = counts.at[:, 0].set(MAXIMG)

    def shuffle_one(single_key):
        return jax.random.permutation(single_key, slot_count)
    shuffles = jax.vmap(shuffle_one)(jax.random.split(order_key, GROUPS))
    first_owner = shuffles[:, 0] // SLOTS
    position = jnp.argsort(shuffles, axis=1)
    numbers = jnp.arange(slot_count)
    ranking = jnp.where(numbers[None, :] // SLOTS == first_owner[:, None], numbers[None, :] % SLOTS, SLOTS + position)
    ordering = jnp.argsort(ranking, axis=1)
    starts = jnp.cumsum(counts, axis=1) - counts
    index = starts[:, :, None] + jnp.arange(MAXIMG)[None, None, :]
    live = jnp.arange(MAXIMG)[None, None, :] < counts[:, :, None]
    picked = jnp.take_along_axis(ordering, jnp.clip(index, 0, slot_count - 1).reshape(GROUPS, -1), axis=1)
    picked = picked.reshape(GROUPS, per_group, MAXIMG)
    spare = jax.random.randint(spare_key, (GROUPS, per_group, MAXIMG), 0, slot_count)
    chosen = jnp.where(live, picked, spare)
    return (counts.reshape(SEQS).astype(jnp.int32), chosen.reshape(SEQS, MAXIMG).astype(jnp.int32))


def draw_image_counts(key, part):
    shared = image_layout(key)
    return shared[0]


def draw_image_slot(key, part):
    shared = image_layout(key)
    return shared[1]


def draw_block_mask(key, part):
    key = jax.random.fold_in(key, 23)
    picks = jax.random.randint(key, (TOKENS, MAXIMG * IMG_BLK), 0, 5)
    marked = (picks < 3).astype(jnp.int32)
    return marked.at[:, 0].set(1)


def draw_key_cache(key, part):
    key = jax.random.fold_in(key, 37)
    base_key = jax.random.fold_in(key, 0)
    shape = (GROUPS, KEYS // BLOCK_TOK, BLOCK_TOK, KVH * HD)
    base = jax.random.truncated_normal(base_key, -6.0, 6.0, shape)
    return base.reshape(GROUPS, KEYS, KVH * HD).astype(jnp.bfloat16)


def block_scale(own_key, extent, shards, smallest, largest):
    def one(axis_at, shards_of):
        steps = jax.random.uniform(jax.random.fold_in(jax.random.fold_in(own_key, 6), axis_at), (shards_of,), jnp.float32, smallest / len(shards), largest / len(shards))
        return jnp.repeat(jnp.exp(steps), extent[axis_at] // shards_of).reshape((-1,) + (1,) * (len(extent) - axis_at - 1))

    level = one(*shards[0])
    for cut in shards[1:]:
        level = level * one(*cut)
    return level


def gaussian(stream_key, dims, spread, reach, cuts=(), held_as=jnp.bfloat16):
    drawn = jax.random.normal(stream_key, dims, jnp.float32) * spread
    if len(cuts) > 0:
        drawn = block_scale(stream_key, dims, cuts, -0.22, 0.18) * drawn
    return jnp.clip(drawn, min=-reach, max=reach).astype(held_as)


def setup_inputs(seed: int = 0) -> dict:
    key_list = jax.random.split(jax.random.key(seed), 12)
    return {
        "tokens": gaussian(key_list[0], (TOKENS, D), 1.0, 6.0, ((0, 64), (1, 8))),
        "norm_gain": jnp.clip(jnp.exp(math.log(2.0) - 1.3862944 * jax.random.uniform(key_list[1], (D,), jnp.float32) ** block_scale(key_list[1], (D,), ((0, 8),), -0.2, 0.2)), 0.5, 2.0),
        "w_query": gaussian(key_list[2], (D, HQ), D ** -0.5, 0.0625, ((0, 8), (1, 64))),
        "query_gain": jnp.clip(jnp.exp(jax.random.uniform(key_list[3], (HD,), jnp.float32, math.log(0.5), math.log(2.0))), 0.5, 2.0),
        "key_cache": draw_key_cache(jax.random.fold_in(key_list[11], 71), 0),
        "value_cache": gaussian(key_list[5], (GROUPS, KEYS, KVH * HD), 8.0, 48.0, ((0, 64), (1, 8))),
        "block_mask": draw_block_mask(jax.random.fold_in(key_list[11], 71), 0),
        "image_counts": draw_image_counts(jax.random.fold_in(key_list[11], 71), 0),
        "image_slot": draw_image_slot(jax.random.fold_in(key_list[11], 71), 0),
        "attn_gate": jnp.clip(jax.random.uniform(key_list[9], (1,), jnp.float32, 0.8, 2.0), 0.8, 2.0),
        "w_out": gaussian(key_list[10], (HQ, D), HQ ** -0.5, 0.0625, ((0, 8), (1, 64))),
    }


NEGATIVE = -1e+30
EPSILON = 1e-05

def reference(tokens, norm_gain, w_query, query_gain, key_cache, value_cache, block_mask, image_counts, image_slot, attn_gate, w_out):
    scaled = (tokens.astype(jnp.float32) * norm_gain).astype(jnp.bfloat16)
    query_raw = jnp.dot(scaled, w_query, preferred_element_type=jnp.float32)
    per_head = query_raw.reshape(TOKENS, H, HD)
    inverse = lax.rsqrt(lax.optimization_barrier(jnp.mean(per_head * per_head, axis=-1, keepdims=True)) + EPSILON)
    query = (per_head * inverse * query_gain).astype(jnp.bfloat16)
    per_group = SEQS // GROUPS
    group_rows = per_group * STEPS
    query_groups = query.reshape(GROUPS, group_rows, KVH, H // KVH, HD)
    mask_groups = block_mask.reshape(GROUPS, group_rows, MAXIMG, IMG_BLK)
    count_groups = image_counts.reshape(GROUPS, per_group)
    slot_groups = image_slot.reshape(GROUPS, per_group, MAXIMG)

    def one_group(items):
        query_four, keys, values, masks, counts, slots = items
        keys = keys.astype(jnp.float32).reshape(KEYS, KVH, HD)
        values = values.astype(jnp.float32).reshape(KEYS, KVH, HD)
        slot_numbers = jnp.arange(KEYS // IMG_TOK, dtype=jnp.int32)
        live = jnp.arange(MAXIMG, dtype=jnp.int32)[None, :] < counts[:, None]
        match = (slots[:, :, None] == slot_numbers[None, None, :]) & live[:, :, None]
        match = jnp.repeat(match, STEPS, axis=0)
        allowed = jnp.any(match[:, :, :, None] & (masks == 1)[:, :, None, :], axis=1)
        allowed = jnp.repeat(allowed.reshape(group_rows, -1), BLOCK_TOK, axis=1)
        scores = jnp.einsum('tkgd,skd->tkgs', query_four.astype(jnp.float32), keys) * HD ** (-0.5)
        visible = allowed[:, None, None, :]
        peak = lax.optimization_barrier(jnp.max(jnp.where(visible, scores, NEGATIVE), axis=-1, keepdims=True))
        expo = jnp.where(visible, jnp.exp(scores - peak), 0.0)
        total = lax.optimization_barrier(jnp.sum(expo, axis=-1))
        rounded = lax.optimization_barrier(expo.astype(jnp.bfloat16))
        weighted = jnp.einsum('tkgs,skd->tkgd', rounded.astype(jnp.float32), values)
        result = weighted / total[..., None]
        return result.astype(jnp.bfloat16).reshape(group_rows, HQ)
    attended = lax.map(one_group, (query_groups, key_cache, value_cache, mask_groups, count_groups, slot_groups))
    attended = attended.reshape(TOKENS, HQ)
    branch = jnp.dot(attended, w_out, preferred_element_type=jnp.float32)
    return (jnp.tanh(attn_gate[0]) * branch).astype(jnp.bfloat16)
```

```python
import functools

import jax
import jax.numpy as jnp
from jax import lax
from jax.experimental import pallas as pl
from jax.experimental.pallas import tpu as pltpu
from jax.sharding import Mesh
from jax.sharding import PartitionSpec as P

H = 64
KVH = 8
HD = 128
IMG_BLK = 4
BLOCK_TOK = 128
IMG_TOK = 512
STEPS = 4

NEGATIVE = -1e30
EPSILON = 1e-05

BF16 = jnp.bfloat16
F32 = jnp.float32
MIB = 1 << 20

AXES = ("j", "s", "y", "x", "c")
SIZES = (8, 2, 4, 4, 2)
ZED = ("j", "s")
IMG = ("x", "c")
FSDP = ("j", "s", "y")
MAIN = 896

SMEM = pl.BlockSpec(memory_space=pltpu.SMEM)


def cost(flops, size, exps=0):
    return pl.CostEstimate(flops=flops, bytes_accessed=size, transcendentals=exps)


def query_product(main, rest, weights):
    def kernel(main_ref, rest_ref, weight_ref, out_ref):
        product = jnp.dot(main_ref[...], weight_ref[0, :MAIN], preferred_element_type=F32)
        product += jnp.dot(
            rest_ref[...].reshape(512, 1024 - MAIN), weight_ref[0, MAIN:], preferred_element_type=F32
        )
        product = product.reshape(16, 4, 8, HD)
        for pair in range(4):
            out_ref[pair] = product[:, pair]

    return pl.pallas_call(
        kernel,
        grid=(4,),
        in_specs=[
            pl.BlockSpec((512, MAIN), lambda n: (0, 0)),
            pl.BlockSpec((16, 32, 1024 - MAIN), lambda n: (0, 0, 0)),
            pl.BlockSpec((1, 1024, HD), lambda n: (n, 0, 0)),
        ],
        out_specs=pl.BlockSpec((4, 16, 8, HD), lambda n: (0, 0, 0, n)),
        out_shape=jax.ShapeDtypeStruct((4, 16, 8, 4 * HD), F32),
        compiler_params=pltpu.CompilerParams(vmem_limit_bytes=24 * MIB),
        cost_estimate=cost(2 * 512 * 1024 * 512, 3 * MIB),
    )(main, rest, weights)


def swap_halves(value):
    return pltpu.roll(value, 4, 1)


def query_norm(mine, other, gain):
    def kernel(mine_ref, other_ref, gain_ref, out_ref):
        heads = []
        for h in range(4):
            columns = slice(h * HD, (h + 1) * HD)
            value = mine_ref[:, :, columns] + other_ref[:, :, columns]
            inverse = lax.rsqrt(jnp.mean(value * value, axis=-1, keepdims=True) + EPSILON)
            heads.append(value * inverse * gain_ref[...].reshape(1, 1, HD))
        low = lax.broadcasted_iota(jnp.int32, (16, 8, HD), 1) < 4
        for h in (0, 2):
            rows = slice(h * 4, h * 4 + 8)
            first = jnp.where(low, heads[h], swap_halves(heads[h + 1]))
            second = jnp.where(low, swap_halves(heads[h]), heads[h + 1])
            out_ref[:, 0, rows] = first.astype(BF16)
            out_ref[:, 1, rows] = second.astype(BF16)

    return pl.pallas_call(
        kernel,
        out_shape=jax.ShapeDtypeStruct((16, 2, 16, HD), BF16),
        compiler_params=pltpu.CompilerParams(vmem_limit_bytes=16 * MIB),
        cost_estimate=cost(1 << 20, MIB),
    )(mine, other, gain)


def attend(place, slots, counts, marks, query, keys, values):
    def kernel(place_ref, slots_ref, counts_ref, marks_ref, query_ref, key_ref, value_ref, out_ref):
        slot = place_ref[0] * 2 + pl.program_id(0)
        sequence, image, used = jnp.int32(0), jnp.int32(0), jnp.int32(0)
        for s in range(8):
            for k in range(2):
                hit = jnp.logical_and(slots_ref[s, k] == slot, k < counts_ref[s])
                sequence = jnp.where(hit, s, sequence)
                image = jnp.where(hit, k, image)
                used = jnp.where(hit, 1, used)

        @pl.when(used == 1)
        def _():
            step = lax.broadcasted_iota(jnp.int32, (8, BLOCK_TOK), 0) % STEPS
            lane = lax.broadcasted_iota(jnp.int32, (8, HD), 1)
            blocks = []
            for b in range(IMG_BLK):
                block = jnp.zeros((8, BLOCK_TOK), jnp.int32)
                for t in range(STEPS):
                    block = jnp.where(step == t, marks_ref[sequence * STEPS + t, image * IMG_BLK + b], block)
                blocks.append(block)
            visible = (jnp.concatenate(blocks, axis=1) == 1).reshape(1, 8, IMG_TOK)
            pair, half = sequence // 2, sequence % 2
            for head in range(KVH):
                columns = slice(head * HD, (head + 1) * HD)
                rows = jnp.concatenate([query_ref[pair, 2 * head, half], query_ref[pair, 2 * head + 1, half]], axis=0)
                scores = lax.dot_general(
                    rows, key_ref[:, columns], (((1,), (1,)), ((), ())), preferred_element_type=F32
                ) * HD ** (-0.5)
                scores = scores.reshape(4, 8, IMG_TOK)
                peak = jnp.max(jnp.where(visible, scores, NEGATIVE), axis=-1, keepdims=True)
                expo = jnp.where(visible, jnp.exp(scores - peak), 0.0)
                total = jnp.sum(expo, axis=-1, keepdims=True)
                out_ref[head, 0, :32] = jnp.dot(
                    expo.astype(BF16).reshape(32, IMG_TOK), value_ref[:, columns], preferred_element_type=F32
                )
                figures = jnp.zeros((8, HD), F32)
                for g in range(4):
                    figures = jnp.where(lane == 2 * g, peak[g], figures)
                    figures = jnp.where(lane == 2 * g + 1, total[g], figures)
                out_ref[head, 0, 32:] = figures

    return pl.pallas_call(
        kernel,
        grid=(2,),
        in_specs=[
            SMEM,
            SMEM,
            SMEM,
            SMEM,
            pl.BlockSpec((4, 16, 2, 16, HD), lambda n: (0, 0, 0, 0, 0)),
            pl.BlockSpec((IMG_TOK, KVH * HD), lambda n: (n, 0)),
            pl.BlockSpec((IMG_TOK, KVH * HD), lambda n: (n, 0)),
        ],
        out_specs=pl.BlockSpec((KVH, 1, 40, HD), lambda n: (0, n, 0, 0)),
        out_shape=jax.ShapeDtypeStruct((KVH, 2, 40, HD), F32),
        compiler_params=pltpu.CompilerParams(vmem_limit_bytes=24 * MIB),
        cost_estimate=cost(4 * 2 * 32 * 8 * 512 * 128, 5 * MIB, 2 * 8 * 32 * 512),
    )(place, slots, counts, marks, query, keys, values)


def merge(slots, counts, pieces):
    def kernel(slots_ref, counts_ref, piece_ref, out_ref):
        low = lax.broadcasted_iota(jnp.int32, (8, HD), 0) < 4
        results = []
        for s in range(8):
            first = jnp.clip(slots_ref[s, 0], 0, 15)
            second = jnp.clip(slots_ref[s, 1], 0, 15)
            both = counts_ref[s] > 1
            result = []
            for g in range(4):
                rows = slice(8 * g, 8 * g + 8)
                peak_first = piece_ref[first, 32:, 2 * g : 2 * g + 1]
                total_first = piece_ref[first, 32:, 2 * g + 1 : 2 * g + 2]
                peak_second = jnp.where(both, piece_ref[second, 32:, 2 * g : 2 * g + 1], NEGATIVE)
                total_second = jnp.where(both, piece_ref[second, 32:, 2 * g + 1 : 2 * g + 2], 0.0)
                weighted_second = jnp.where(both, piece_ref[second, rows], 0.0)
                peak = jnp.maximum(peak_first, peak_second)
                factor_first = jnp.exp(peak_first - peak)
                factor_second = jnp.exp(peak_second - peak)
                total = total_first * factor_first + total_second * factor_second
                result.append((piece_ref[first, rows] * factor_first + weighted_second * factor_second) / total)
            results.append(result)
        for h in range(8):
            tiles = []
            for pair in range(4):
                even, odd = results[2 * pair][h // 2], results[2 * pair + 1][h // 2]
                if h % 2 == 0:
                    tiles.append(jnp.where(low, even, pltpu.roll(odd, 4, 0)))
                else:
                    tiles.append(jnp.where(low, pltpu.roll(even, 4, 0), odd))
            out_ref[:, h * HD : (h + 1) * HD] = jnp.concatenate(tiles, axis=0).astype(BF16)

    return pl.pallas_call(
        kernel,
        in_specs=[SMEM, SMEM, pl.BlockSpec(memory_space=pltpu.VMEM)],
        out_shape=jax.ShapeDtypeStruct((32, KVH * HD), BF16),
        compiler_params=pltpu.CompilerParams(vmem_limit_bytes=16 * MIB),
        cost_estimate=cost(1 << 18, MIB // 2, 2048),
    )(slots, counts, pieces)


def out_product(attended, weights):
    def kernel(attended_ref, weight_ref, out_ref):
        product = jnp.dot(attended_ref[...].reshape(256, 1024), weight_ref[0], preferred_element_type=F32)
        product = product.reshape(4, 2, 32, HD)
        for s in range(2):
            out_ref[0, s] = product[:, s]

    return pl.pallas_call(
        kernel,
        grid=(8,),
        in_specs=[
            pl.BlockSpec((4, 2, 32, 1024), lambda n: (0, 0, 0, 0)),
            pl.BlockSpec((1, 1024, HD), lambda n: (n, 0, 0)),
        ],
        out_specs=pl.BlockSpec((1, 2, 4, 32, HD), lambda n: (n, 0, 0, 0, 0)),
        out_shape=jax.ShapeDtypeStruct((8, 2, 4, 32, HD), F32),
        compiler_params=pltpu.CompilerParams(vmem_limit_bytes=24 * MIB),
        cost_estimate=cost(2 * 256 * 1024 * 1024, 4 * MIB),
    )(attended, weights)


def on_device(
    tokens,
    norm_gain,
    w_query,
    query_gain,
    key_cache,
    value_cache,
    block_mask,
    image_counts,
    image_slot,
    attn_gate,
    w_out,
):
    core = lax.axis_index("c")
    place = (lax.axis_index("x") * 2 + core).reshape(1)
    swap = [(0, 1), (1, 0)]

    query_weights = lax.all_gather(w_query, "y")
    query_weights, w_out = lax.optimization_barrier((query_weights, w_out))
    out_weights = lax.all_gather(w_out, "j")

    scaled = (tokens.astype(F32) * norm_gain).astype(BF16)
    rest = jnp.broadcast_to(scaled[None, :, MAIN:], (16, 32, 1024 - MAIN))
    rest = lax.all_to_all(rest, ZED, 0, 0, tiled=True)
    main = lax.all_gather(scaled[:, :MAIN], ZED, axis=0, tiled=True)

    partial = query_product(main, rest, query_weights)
    partial = jnp.sum(lax.all_to_all(partial, "x", 0, 0, tiled=True).reshape(4, 16, 8, 512), axis=0)
    query = query_norm(partial, lax.ppermute(partial, "c", swap), query_gain.reshape(1, HD))
    query = lax.all_to_all(query, ZED, 0, 0, tiled=True)
    query = lax.all_gather(query, "x")

    pieces = attend(place, image_slot, image_counts, block_mask, query, key_cache[0], value_cache[0])
    pieces = lax.all_to_all(pieces, IMG, 0, 0, tiled=True).reshape(16, 40, HD)
    attended = merge(image_slot, image_counts, pieces)

    attended = lax.all_gather(lax.all_gather(attended, "s"), "y")
    partial = out_product(attended, out_weights).reshape(4, 2, 256, HD)
    partial = lax.all_to_all(partial, "x", 0, 0, tiled=True).reshape(4, 2, 256, HD)
    other = jnp.sum(lax.dynamic_index_in_dim(partial, 1 - core, 1, keepdims=False), axis=0)
    other = lax.ppermute(other, "c", swap)
    own = jnp.sum(lax.dynamic_index_in_dim(partial, core, 1, keepdims=False), axis=0)
    mixed = (jnp.tanh(attn_gate[0]) * (own + other)).astype(BF16)
    turn = [(a * 8 + b, b * 8 + a) for a in range(8) for b in range(8)]
    return lax.ppermute(mixed, ("j",) + IMG, turn)


def solution(mesh):
    fine = Mesh(mesh.devices.reshape(SIZES), AXES)
    placed = (
        P(FSDP, IMG),
        P(IMG),
        P(IMG, FSDP),
        P(),
        P(FSDP, IMG, None),
        P(FSDP, IMG, None),
        P(FSDP, None),
        P(FSDP),
        P(FSDP, None),
        P(),
        P(IMG, FSDP),
    )
    return jax.shard_map(on_device, mesh=fine, in_specs=placed, out_specs=P(IMG, FSDP), check_vma=False)
```

```python
import functools

import jax
import jax.numpy as jnp
from jax import lax
from jax.experimental import pallas as pl
from jax.experimental.pallas import tpu as pltpu
from jax.sharding import Mesh
from jax.sharding import PartitionSpec as P

H = 64
KVH = 8
HD = 128
IMG_BLK = 4
BLOCK_TOK = 128
IMG_TOK = 512
STEPS = 4

NEGATIVE = -1e30
EPSILON = 1e-05

BF16 = jnp.bfloat16
F32 = jnp.float32
MIB = 1 << 20

AXES = ("j", "s", "y", "x", "c")
SIZES = (8, 2, 4, 4, 2)
ZED = ("j", "s")
IMG = ("x", "c")
FSDP = ("j", "s", "y")
MAIN = 896

SMEM = pl.BlockSpec(memory_space=pltpu.SMEM)


def cost(flops, size, exps=0):
    return pl.CostEstimate(flops=flops, bytes_accessed=size, transcendentals=exps)


def query_product(main, rest, weights):
    def kernel(main_ref, rest_ref, weight_ref, out_ref):
        weight = jnp.concatenate([weight_ref[0], weight_ref[1]], axis=1)
        product = jnp.dot(main_ref[...], weight[:MAIN], preferred_element_type=F32)
        product += jnp.dot(rest_ref[...].reshape(512, 1024 - MAIN), weight[MAIN:], preferred_element_type=F32)
        product = product.reshape(16, 4, 8, 2 * HD)
        for pair in range(4):
            out_ref[pair] = product[:, pair]

    return pl.pallas_call(
        kernel,
        grid=(2,),
        in_specs=[
            pl.BlockSpec((512, MAIN), lambda n: (0, 0)),
            pl.BlockSpec((16, 32, 1024 - MAIN), lambda n: (0, 0, 0)),
            pl.BlockSpec((2, 1024, HD), lambda n: (n, 0, 0)),
        ],
        out_specs=pl.BlockSpec((4, 16, 8, 2 * HD), lambda n: (0, 0, 0, n)),
        out_shape=jax.ShapeDtypeStruct((4, 16, 8, 4 * HD), F32),
        compiler_params=pltpu.CompilerParams(vmem_limit_bytes=24 * MIB),
        cost_estimate=cost(2 * 512 * 1024 * 512, 3 * MIB),
    )(main, rest, weights)


def swap_halves(value):
    return pltpu.roll(value, 4, 1)


def query_norm(mine, other, gain):
    def kernel(mine_ref, other_ref, gain_ref, out_ref):
        heads = []
        for h in range(4):
            columns = slice(h * HD, (h + 1) * HD)
            value = mine_ref[:, :, columns] + other_ref[:, :, columns]
            inverse = lax.rsqrt(jnp.mean(value * value, axis=-1, keepdims=True) + EPSILON)
            heads.append(value * inverse * gain_ref[...].reshape(1, 1, HD))
        low = lax.broadcasted_iota(jnp.int32, (16, 8, HD), 1) < 4
        for h in (0, 2):
            rows = slice(h * 4, h * 4 + 8)
            first = jnp.where(low, heads[h], swap_halves(heads[h + 1]))
            second = jnp.where(low, swap_halves(heads[h]), heads[h + 1])
            out_ref[:, 0, rows] = first.astype(BF16)
            out_ref[:, 1, rows] = second.astype(BF16)

    return pl.pallas_call(
        kernel,
        out_shape=jax.ShapeDtypeStruct((16, 2, 16, HD), BF16),
        compiler_params=pltpu.CompilerParams(vmem_limit_bytes=16 * MIB),
        cost_estimate=cost(1 << 20, MIB),
    )(mine, other, gain)


def attend(place, slots, counts, marks, query, keys, values):
    def kernel(place_ref, slots_ref, counts_ref, marks_ref, query_ref, key_ref, value_ref, out_ref):
        slot = place_ref[0] * 2 + pl.program_id(0)
        sequence, image, used = jnp.int32(0), jnp.int32(0), jnp.int32(0)
        for s in range(8):
            for k in range(2):
                hit = jnp.logical_and(slots_ref[s, k] == slot, k < counts_ref[s])
                sequence = jnp.where(hit, s, sequence)
                image = jnp.where(hit, k, image)
                used = jnp.where(hit, 1, used)

        @pl.when(used == 1)
        def _():
            step = lax.broadcasted_iota(jnp.int32, (8, BLOCK_TOK), 0) % STEPS
            lane = lax.broadcasted_iota(jnp.int32, (8, HD), 1)
            blocks = []
            for b in range(IMG_BLK):
                block = jnp.zeros((8, BLOCK_TOK), jnp.int32)
                for t in range(STEPS):
                    block = jnp.where(step == t, marks_ref[sequence * STEPS + t, image * IMG_BLK + b], block)
                blocks.append(block)
            visible = (jnp.concatenate(blocks, axis=1) == 1).reshape(1, 8, IMG_TOK)
            pair, half = sequence // 2, sequence % 2
            for head in range(KVH):
                columns = slice(head * HD, (head + 1) * HD)
                rows = jnp.concatenate([query_ref[pair, 2 * head, half], query_ref[pair, 2 * head + 1, half]], axis=0)
                scores = lax.dot_general(
                    rows, key_ref[:, columns], (((1,), (1,)), ((), ())), preferred_element_type=F32
                ) * HD ** (-0.5)
                scores = scores.reshape(4, 8, IMG_TOK)
                peak = jnp.max(jnp.where(visible, scores, NEGATIVE), axis=-1, keepdims=True)
                expo = jnp.where(visible, jnp.exp(scores - peak), 0.0)
                total = jnp.sum(expo, axis=-1, keepdims=True)
                out_ref[head, 0, :32] = jnp.dot(
                    expo.astype(BF16).reshape(32, IMG_TOK), value_ref[:, columns], preferred_element_type=F32
                )
                figures = jnp.zeros((8, HD), F32)
                for g in range(4):
                    figures = jnp.where(lane == 2 * g, peak[g], figures)
                    figures = jnp.where(lane == 2 * g + 1, total[g], figures)
                out_ref[head, 0, 32:] = figures

    return pl.pallas_call(
        kernel,
        grid=(2,),
        in_specs=[
            SMEM,
            SMEM,
            SMEM,
            SMEM,
            pl.BlockSpec((4, 16, 2, 16, HD), lambda n: (0, 0, 0, 0, 0)),
            pl.BlockSpec((IMG_TOK, KVH * HD), lambda n: (n, 0)),
            pl.BlockSpec((IMG_TOK, KVH * HD), lambda n: (n, 0)),
        ],
        out_specs=pl.BlockSpec((KVH, 1, 40, HD), lambda n: (0, n, 0, 0)),
        out_shape=jax.ShapeDtypeStruct((KVH, 2, 40, HD), F32),
        compiler_params=pltpu.CompilerParams(vmem_limit_bytes=24 * MIB),
        cost_estimate=cost(4 * 2 * 32 * 8 * 512 * 128, 5 * MIB, 2 * 8 * 32 * 512),
    )(place, slots, counts, marks, query, keys, values)


def merge(slots, counts, pieces):
    def kernel(slots_ref, counts_ref, piece_ref, out_ref):
        low = lax.broadcasted_iota(jnp.int32, (8, HD), 0) < 4
        results = []
        for s in range(8):
            first = jnp.clip(slots_ref[s, 0], 0, 15)
            second = jnp.clip(slots_ref[s, 1], 0, 15)
            both = counts_ref[s] > 1
            result = []
            for g in range(4):
                rows = slice(8 * g, 8 * g + 8)
                peak_first = piece_ref[first, 32:, 2 * g : 2 * g + 1]
                total_first = piece_ref[first, 32:, 2 * g + 1 : 2 * g + 2]
                peak_second = jnp.where(both, piece_ref[second, 32:, 2 * g : 2 * g + 1], NEGATIVE)
                total_second = jnp.where(both, piece_ref[second, 32:, 2 * g + 1 : 2 * g + 2], 0.0)
                weighted_second = jnp.where(both, piece_ref[second, rows], 0.0)
                peak = jnp.maximum(peak_first, peak_second)
                factor_first = jnp.exp(peak_first - peak)
                factor_second = jnp.exp(peak_second - peak)
                total = total_first * factor_first + total_second * factor_second
                result.append((piece_ref[first, rows] * factor_first + weighted_second * factor_second) / total)
            results.append(result)
        for h in range(8):
            tiles = []
            for pair in range(4):
                even, odd = results[2 * pair][h // 2], results[2 * pair + 1][h // 2]
                if h % 2 == 0:
                    tiles.append(jnp.where(low, even, pltpu.roll(odd, 4, 0)))
                else:
                    tiles.append(jnp.where(low, pltpu.roll(even, 4, 0), odd))
            tile = jnp.concatenate(tiles, axis=0).astype(BF16)
            for copy in range(8):
                out_ref[copy, :, h * HD : (h + 1) * HD] = tile

    return pl.pallas_call(
        kernel,
        in_specs=[SMEM, SMEM, pl.BlockSpec(memory_space=pltpu.VMEM)],
        out_shape=jax.ShapeDtypeStruct((8, 32, KVH * HD), BF16),
        compiler_params=pltpu.CompilerParams(vmem_limit_bytes=16 * MIB),
        cost_estimate=cost(1 << 18, MIB // 2, 2048),
    )(slots, counts, pieces)


def out_product(attended, weights):
    def kernel(attended_ref, weight_ref, out_ref):
        weight = jnp.concatenate([weight_ref[0], weight_ref[1]], axis=1)
        product = jnp.dot(attended_ref[...], weight, preferred_element_type=F32)
        out_ref[0] = product[:, :HD]
        out_ref[1] = product[:, HD:]

    return pl.pallas_call(
        kernel,
        grid=(4,),
        in_specs=[
            pl.BlockSpec((256, 1024), lambda n: (0, 0)),
            pl.BlockSpec((2, 1024, HD), lambda n: (n, 0, 0)),
        ],
        out_specs=pl.BlockSpec((2, 256, HD), lambda n: (n, 0, 0)),
        out_shape=jax.ShapeDtypeStruct((8, 256, HD), F32),
        compiler_params=pltpu.CompilerParams(vmem_limit_bytes=24 * MIB),
        cost_estimate=cost(2 * 256 * 1024 * 1024, 4 * MIB),
    )(attended, weights)


def on_device(
    tokens,
    norm_gain,
    w_query,
    query_gain,
    key_cache,
    value_cache,
    block_mask,
    image_counts,
    image_slot,
    attn_gate,
    w_out,
):
    core = lax.axis_index("c")
    place = (lax.axis_index("x") * 2 + core).reshape(1)
    swap = [(0, 1), (1, 0)]

    query_weights = lax.all_gather(w_query, "y")
    scaled = (tokens.astype(F32) * norm_gain).astype(BF16)
    rest = jnp.broadcast_to(scaled[None, :, MAIN:], (16, 32, 1024 - MAIN))
    rest = lax.all_to_all(rest, ZED, 0, 0, tiled=True)
    main = lax.all_gather(scaled[:, :MAIN], ZED, axis=0, tiled=True)
    main, w_out = lax.optimization_barrier((main, w_out))
    out_weights = lax.all_gather(w_out, "j")

    partial = query_product(main, rest, query_weights)
    partial = jnp.sum(lax.all_to_all(partial, "x", 0, 0, tiled=True).reshape(4, 16, 8, 512), axis=0)
    query = query_norm(partial, lax.ppermute(partial, "c", swap), query_gain.reshape(1, HD))
    query = lax.all_to_all(query, ZED, 0, 0, tiled=True)
    query = lax.all_to_all(jnp.broadcast_to(query, (4, 16, 2, 16, HD)), "x", 0, 0, tiled=True)

    pieces = attend(place, image_slot, image_counts, block_mask, query, key_cache[0], value_cache[0])
    pieces = lax.all_to_all(pieces, IMG, 0, 0, tiled=True).reshape(16, 40, HD)
    attended = merge(image_slot, image_counts, pieces)

    attended = lax.all_to_all(attended, ("s", "y"), 0, 0, tiled=True).reshape(256, 1024)
    partial = out_product(attended, out_weights).reshape(4, 2, 256, HD)
    partial = lax.all_to_all(partial, "x", 0, 0, tiled=True).reshape(4, 2, 256, HD)
    other = jnp.sum(lax.dynamic_index_in_dim(partial, 1 - core, 1, keepdims=False), axis=0)
    other = lax.ppermute(other, "c", swap)
    own = jnp.sum(lax.dynamic_index_in_dim(partial, core, 1, keepdims=False), axis=0)
    mixed = (jnp.tanh(attn_gate[0]) * (own + other)).astype(BF16)
    turn = [(a * 8 + b, b * 8 + a) for a in range(8) for b in range(8)]
    return lax.ppermute(mixed, ("j",) + IMG, turn)


def solution(mesh):
    fine = Mesh(mesh.devices.reshape(SIZES), AXES)
    placed = (
        P(FSDP, IMG),
        P(IMG),
        P(IMG, FSDP),
        P(),
        P(FSDP, IMG, None),
        P(FSDP, IMG, None),
        P(FSDP, None),
        P(FSDP),
        P(FSDP, None),
        P(),
        P(IMG, FSDP),
    )
    return jax.shard_map(on_device, mesh=fine, in_specs=placed, out_specs=P(IMG, FSDP), check_vma=False)
```

```python
import functools

import jax
import jax.numpy as jnp
from jax import lax
from jax.experimental import pallas as pl
from jax.experimental.pallas import tpu as pltpu
from jax.sharding import Mesh
from jax.sharding import PartitionSpec as P

H = 64
KVH = 8
HD = 128
IMG_BLK = 4
BLOCK_TOK = 128
IMG_TOK = 512
STEPS = 4

NEGATIVE = -1e30
EPSILON = 1e-05

BF16 = jnp.bfloat16
F32 = jnp.float32
MIB = 1 << 20

AXES = ("j", "s", "y", "x", "c")
SIZES = (8, 2, 4, 4, 2)
NEAR = ("s", "y")
IMG = ("x", "c")
FSDP = ("j", "s", "y")

SMEM = pl.BlockSpec(memory_space=pltpu.SMEM)


def cost(flops, size, exps=0):
    return pl.CostEstimate(flops=flops, bytes_accessed=size, transcendentals=exps)


def product(rows, weights, kept):
    def kernel(rows_ref, weight_ref, out_ref):
        weight = jnp.concatenate([weight_ref[0], weight_ref[1]], axis=1)
        total = jnp.dot(rows_ref[...], weight, preferred_element_type=F32)
        out_ref[0] = total[:, :HD].astype(kept)
        out_ref[1] = total[:, HD:].astype(kept)

    return pl.pallas_call(
        kernel,
        grid=(4,),
        in_specs=[
            pl.BlockSpec((256, 1024), lambda n: (0, 0)),
            pl.BlockSpec((2, 1024, HD), lambda n: (n, 0, 0)),
        ],
        out_specs=pl.BlockSpec((2, 256, HD), lambda n: (n, 0, 0)),
        out_shape=jax.ShapeDtypeStruct((8, 256, HD), kept),
        compiler_params=pltpu.CompilerParams(vmem_limit_bytes=24 * MIB),
        cost_estimate=cost(2 * 256 * 1024 * 1024, 4 * MIB),
    )(rows, weights)


def query_norm(parts, gain):
    def kernel(part_ref, gain_ref, out_ref):
        value = jnp.sum(part_ref[...], axis=0)
        inverse = lax.rsqrt(jnp.mean(value * value, axis=-1, keepdims=True) + EPSILON)
        out_ref[...] = (value * inverse * gain_ref[...]).astype(BF16)

    return pl.pallas_call(
        kernel,
        out_shape=jax.ShapeDtypeStruct((256, HD), BF16),
        compiler_params=pltpu.CompilerParams(vmem_limit_bytes=16 * MIB),
        cost_estimate=cost(1 << 18, MIB // 4),
    )(parts, gain)


def attend(slots, counts, marks, query, caches):
    def kernel(slots_ref, counts_ref, marks_ref, query_ref, cache_ref, out_ref):
        step = lax.broadcasted_iota(jnp.int32, (8, BLOCK_TOK), 0) % STEPS
        low = lax.broadcasted_iota(jnp.int32, (8, HD), 0) < 4
        heads = [query_ref[h % 4 * 2 + h // 4].astype(F32) for h in range(8)]
        results = []
        for s in range(8):
            blocks, scores, places = [], [], []
            tiles = []
            for h in range(0, 8, 2):
                even, odd = (head[s // 2 * 8 : s // 2 * 8 + 8] for head in heads[h : h + 2])
                if s % 2 == 0:
                    tiles.append(jnp.where(low, even, pltpu.roll(odd, 4, 0)))
                else:
                    tiles.append(jnp.where(low, pltpu.roll(even, 4, 0), odd))
            rows = jnp.concatenate(tiles, axis=0).astype(BF16)
            for k in range(2):
                slot = jnp.clip(slots_ref[s, k], 0, 15)
                places.append((slot // 2, slot % 2))
                live = (k < counts_ref[s]).astype(jnp.int32)
                for b in range(IMG_BLK):
                    block = jnp.zeros((8, BLOCK_TOK), jnp.int32)
                    for t in range(STEPS):
                        block = jnp.where(step == t, marks_ref[s * STEPS + t, k * IMG_BLK + b] * live, block)
                    blocks.append(block)
                scores.append(
                    lax.dot_general(
                        rows,
                        cache_ref[places[k][0], 0, places[k][1]],
                        (((1,), (1,)), ((), ())),
                        preferred_element_type=F32,
                    )
                )
            visible = (jnp.concatenate(blocks, axis=1) == 1).reshape(1, 8, 2 * IMG_TOK)
            score = (jnp.concatenate(scores, axis=1) * HD ** (-0.5)).reshape(4, 8, 2 * IMG_TOK)
            peak = jnp.max(jnp.where(visible, score, NEGATIVE), axis=-1, keepdims=True)
            expo = jnp.where(visible, jnp.exp(score - peak), 0.0)
            total = jnp.sum(expo, axis=-1, keepdims=True)
            expo = expo.astype(BF16).reshape(32, 2 * IMG_TOK)
            weighted = jnp.dot(
                expo[:, :IMG_TOK], cache_ref[places[0][0], 1, places[0][1]], preferred_element_type=F32
            ) + jnp.dot(expo[:, IMG_TOK:], cache_ref[places[1][0], 1, places[1][1]], preferred_element_type=F32)
            results.append(weighted.reshape(4, 8, HD) / total)
        for h in range(8):
            tiles = []
            for pair in range(4):
                even, odd = results[2 * pair][h // 2], results[2 * pair + 1][h // 2]
                if h % 2 == 0:
                    tiles.append(jnp.where(low, even, pltpu.roll(odd, 4, 0)))
                else:
                    tiles.append(jnp.where(low, pltpu.roll(even, 4, 0), odd))
            tile = jnp.concatenate(tiles, axis=0).astype(BF16)
            out_ref[:, h * HD : (h + 1) * HD] = tile

    whole = pl.BlockSpec(memory_space=pltpu.VMEM)
    return pl.pallas_call(
        kernel,
        in_specs=[SMEM, SMEM, SMEM, whole, whole],
        out_specs=whole,
        out_shape=jax.ShapeDtypeStruct((32, KVH * HD), BF16),
        compiler_params=pltpu.CompilerParams(vmem_limit_bytes=24 * MIB),
        cost_estimate=cost(4 * 2 * 32 * 8 * 512 * 128, 5 * MIB, 2 * 8 * 32 * 512),
    )(slots, counts, marks, query, caches)


def on_device(
    tokens,
    norm_gain,
    w_query,
    query_gain,
    key_cache,
    value_cache,
    block_mask,
    image_counts,
    image_slot,
    attn_gate,
    w_out,
):
    query_weights = lax.all_gather(w_query, "j")
    caches = jnp.stack([key_cache[0], value_cache[0]]).reshape(2, 1024, KVH, HD).transpose(2, 0, 1, 3)
    caches, tokens = lax.optimization_barrier((caches, tokens))
    caches = lax.all_to_all(caches, IMG, 0, 0, tiled=True)
    scaled = (tokens.astype(F32) * norm_gain).astype(BF16)
    scaled = lax.all_gather(lax.all_gather(scaled, "s"), "y")

    partial = product(scaled.reshape(256, 1024), query_weights, F32).reshape(4, 2, 256, HD)
    partial, caches, w_out = lax.optimization_barrier((partial, caches, w_out))
    out_weights = lax.all_gather(w_out, NEAR)
    partial = lax.all_to_all(partial.reshape(8, 256, HD), IMG, 0, 0, tiled=True)
    query = query_norm(partial, query_gain.reshape(1, HD))
    query = lax.all_to_all(query.reshape(8, 32, HD), ("y", "s"), 0, 0, tiled=True)
    attended = attend(image_slot, image_counts, block_mask, query, caches.reshape(8, 2, 2, IMG_TOK, HD))

    attended = lax.all_gather(attended, "j", axis=0, tiled=True)
    partial = product(attended, out_weights, BF16).reshape(64, 32, HD)
    partial = lax.all_to_all(partial, NEAR + IMG, 0, 0, tiled=True).reshape(8, 8, 32, HD)
    return (jnp.tanh(attn_gate[0]) * jnp.sum(partial.astype(F32), axis=1)).astype(BF16).reshape(256, HD)


def solution(mesh):
    fine = Mesh(mesh.devices.reshape(SIZES), AXES)
    placed = (
        P(FSDP, IMG),
        P(IMG),
        P(IMG, FSDP),
        P(),
        P(FSDP, IMG, None),
        P(FSDP, IMG, None),
        P(FSDP, None),
        P(FSDP),
        P(FSDP, None),
        P(),
        P(IMG, FSDP),
    )
    return jax.shard_map(on_device, mesh=fine, in_specs=placed, out_specs=P(IMG, FSDP), check_vma=False)
```

```python
import functools

import jax
import jax.numpy as jnp
from jax import lax
from jax.experimental import pallas as pl
from jax.experimental.pallas import tpu as pltpu
from jax.sharding import Mesh
from jax.sharding import PartitionSpec as P

H = 64
KVH = 8
HD = 128
IMG_BLK = 4
BLOCK_TOK = 128
IMG_TOK = 512
STEPS = 4

NEGATIVE = -1e30
EPSILON = 1e-05

BF16 = jnp.bfloat16
F32 = jnp.float32
MIB = 1 << 20

AXES = ("j", "s", "y", "x", "c")
SIZES = (8, 2, 4, 4, 2)
NEAR = ("s", "y")
IMG = ("x", "c")
FSDP = ("j", "s", "y")

SMEM = pl.BlockSpec(memory_space=pltpu.SMEM)


def cost(flops, size, exps=0):
    return pl.CostEstimate(flops=flops, bytes_accessed=size, transcendentals=exps)


def query_product(core, rows, weights):
    def kernel(core_ref, rows_ref, weight_ref, own_ref, other_ref):
        value = rows_ref[...].reshape(256, 1024)
        for pair in range(4):
            weight = jnp.concatenate([weight_ref[2 * pair], weight_ref[2 * pair + 1]], axis=1)
            total = jnp.dot(value, weight, preferred_element_type=F32).reshape(8, 32, 2 * HD)
            first, second = total[:, :, :HD], total[:, :, HD:]
            own_ref[:, pair] = jnp.where(core_ref[0] == 0, first, second)
            other_ref[:, pair] = jnp.where(core_ref[0] == 0, second, first)

    shape = jax.ShapeDtypeStruct((8, 4, 32, HD), F32)
    whole = pl.BlockSpec(memory_space=pltpu.VMEM)
    return pl.pallas_call(
        kernel,
        in_specs=[SMEM, whole, whole],
        out_specs=[whole, whole],
        out_shape=(shape, shape),
        compiler_params=pltpu.CompilerParams(vmem_limit_bytes=24 * MIB),
        cost_estimate=cost(2 * 256 * 1024 * 1024, 4 * MIB),
    )(core, rows, weights)


def out_product(core, spot, rows, weights):
    def kernel(core_ref, spot_ref, rows_ref, *refs):
        *weight_refs, own_ref, other_ref = refs
        value = rows_ref[...].reshape(256, 1024)
        for back, weight_ref in enumerate(weight_refs):
            weight = jnp.concatenate([weight_ref[0], weight_ref[1]], axis=1)
            total = jnp.dot(value, weight, preferred_element_type=F32).reshape(4, 2, 32, 2 * HD)
            own = jnp.where(core_ref[0] == 0, total[:, 0], total[:, 1])
            other = jnp.where(core_ref[0] == 0, total[:, 1], total[:, 0])
            place = lax.rem(spot_ref[0] + 4 - back, 4)
            for s in range(2):
                own_ref[place, s] = own[:, :, s * HD : (s + 1) * HD]
                other_ref[place, s] = other[:, :, s * HD : (s + 1) * HD]

    shape = jax.ShapeDtypeStruct((4, 2, 4, 32, HD), F32)
    whole = pl.BlockSpec(memory_space=pltpu.VMEM)
    return pl.pallas_call(
        kernel,
        in_specs=[SMEM, SMEM] + [whole] * 5,
        out_specs=[whole, whole],
        out_shape=(shape, shape),
        compiler_params=pltpu.CompilerParams(vmem_limit_bytes=24 * MIB),
        cost_estimate=cost(2 * 256 * 1024 * 1024, 4 * MIB),
    )(core, spot, rows, *weights)


def attend(slots, marks, parts, gain, caches):
    def kernel(slots_ref, marks_ref, part_ref, gain_ref, cache_ref, out_ref, score_ref, expo_ref):
        low = lax.broadcasted_iota(jnp.int32, (8, HD), 0) < 4
        places = []
        for s in range(8):
            slot = [jnp.clip(slots_ref[s, k], 0, 15) for k in range(2)]
            places.append([(one // 2, one % 2) for one in slot])
        heads = []
        for h in range(8):
            value = jnp.sum(part_ref[h % 4 * 2 + h // 4], axis=0)
            inverse = lax.rsqrt(jnp.mean(value * value, axis=-1, keepdims=True) + EPSILON)
            heads.append(value * inverse * gain_ref[...])
        for s in range(8):
            tiles = []
            for h in range(0, 8, 2):
                even, odd = (head[s // 2 * 8 : s // 2 * 8 + 8] for head in heads[h : h + 2])
                if s % 2 == 0:
                    tiles.append(jnp.where(low, even, pltpu.roll(odd, 4, 0)))
                else:
                    tiles.append(jnp.where(low, pltpu.roll(even, 4, 0), odd))
            rows = jnp.concatenate(tiles, axis=0).astype(BF16)
            for k in range(2):
                score_ref[s, :, k * IMG_TOK : (k + 1) * IMG_TOK] = lax.dot_general(
                    rows,
                    cache_ref[places[s][k][0], 0, places[s][k][1]],
                    (((1,), (1,)), ((), ())),
                    preferred_element_type=F32,
                )
        totals = []
        for s in range(8):
            blocks = [
                jnp.broadcast_to(marks_ref[8 * s : 8 * s + 8, b : b + 1], (8, BLOCK_TOK)) for b in range(2 * IMG_BLK)
            ]
            visible = (jnp.concatenate(blocks, axis=1) > 0.5).reshape(1, 8, 2 * IMG_TOK)
            score = (score_ref[s] * HD ** (-0.5)).reshape(4, 8, 2 * IMG_TOK)
            peak = jnp.max(jnp.where(visible, score, NEGATIVE), axis=-1, keepdims=True)
            expo = jnp.where(visible, jnp.exp(score - peak), 0.0)
            totals.append(jnp.sum(expo, axis=-1, keepdims=True))
            expo_ref[s] = expo.reshape(32, 2 * IMG_TOK).astype(BF16)
        results = []
        for s in range(8):
            first, second = (cache_ref[place[0], 1, place[1]] for place in places[s])
            weighted = jnp.dot(expo_ref[s, :, :IMG_TOK], first, preferred_element_type=F32)
            weighted += jnp.dot(expo_ref[s, :, IMG_TOK:], second, preferred_element_type=F32)
            results.append(weighted.reshape(4, 8, HD) / totals[s])
        for h in range(8):
            tiles = []
            for pair in range(4):
                even, odd = results[2 * pair][h // 2], results[2 * pair + 1][h // 2]
                if h % 2 == 0:
                    tiles.append(jnp.where(low, even, pltpu.roll(odd, 4, 0)))
                else:
                    tiles.append(jnp.where(low, pltpu.roll(even, 4, 0), odd))
            tile = jnp.concatenate(tiles, axis=0).astype(BF16)
            out_ref[:, h * HD : (h + 1) * HD] = tile

    whole = pl.BlockSpec(memory_space=pltpu.VMEM)
    return pl.pallas_call(
        kernel,
        in_specs=[SMEM, whole, whole, whole, whole],
        out_specs=whole,
        out_shape=jax.ShapeDtypeStruct((32, KVH * HD), BF16),
        scratch_shapes=[pltpu.VMEM((8, 32, 2 * IMG_TOK), F32), pltpu.VMEM((8, 32, 2 * IMG_TOK), BF16)],
        compiler_params=pltpu.CompilerParams(vmem_limit_bytes=24 * MIB),
        cost_estimate=cost(4 * 2 * 32 * 8 * 512 * 128, 5 * MIB, 2 * 8 * 32 * 512),
    )(slots, marks, parts, gain, caches)


def on_device(
    tokens,
    norm_gain,
    w_query,
    query_gain,
    key_cache,
    value_cache,
    block_mask,
    image_counts,
    image_slot,
    attn_gate,
    w_out,
):
    query_weights = lax.all_gather(w_query, "j")
    caches = jnp.stack([key_cache[0], value_cache[0]]).reshape(2, 1024, KVH, HD).transpose(2, 0, 1, 3)
    caches, tokens = lax.optimization_barrier((caches, tokens))
    caches = lax.all_to_all(caches, IMG, 0, 0, tiled=True)
    scaled = (tokens.astype(F32) * norm_gain).astype(BF16)
    scaled = lax.all_gather(lax.all_gather(scaled, "s"), "y")
    out_weights = [lax.all_gather(w_out, "s")]
    for ahead in range(1, 4):
        out_weights.append(lax.ppermute(out_weights[0], "y", [(a, (a + ahead) % 4) for a in range(4)]))
    live = jnp.arange(2, dtype=jnp.int32)[None, :] < image_counts[:, None]
    marks = (block_mask.reshape(8, STEPS, 2, IMG_BLK) == 1) & live[:, None, :, None]
    marks = jnp.tile(marks.reshape(8, STEPS, 2 * IMG_BLK).astype(F32), (1, 2, 1)).reshape(64, 2 * IMG_BLK)
    scaled, out_weights, marks = lax.optimization_barrier((scaled, out_weights, marks))

    core = lax.axis_index("c").reshape(1)
    swap = [(0, 1), (1, 0)]
    own, other = query_product(core, scaled.reshape(8, 32, 1024), query_weights)
    own, caches = lax.optimization_barrier((own, caches))
    parts = (own + lax.ppermute(other, "c", swap)).reshape(32, 32, HD)
    parts = lax.all_to_all(parts, ("y", "s", "x"), 0, 0, tiled=True).reshape(8, 4, 32, HD)
    caches = caches.reshape(8, 2, 2, IMG_TOK, HD)
    attended = attend(image_slot, marks, parts, query_gain.reshape(1, HD), caches)

    spot = lax.axis_index("y").reshape(1)
    own, other = out_product(core, spot, lax.all_gather(attended, "j"), out_weights)
    partial = (own + lax.ppermute(other, "c", swap)).astype(BF16).reshape(32, 32, HD)
    partial = lax.all_to_all(partial, ("y", "s", "x"), 0, 0, tiled=True).reshape(4, 2, 4, 32, HD)
    mixed = (jnp.tanh(attn_gate[0]) * jnp.sum(partial.astype(F32), axis=2)).astype(BF16)
    return mixed.swapaxes(0, 1).reshape(256, HD)


def solution(mesh):
    fine = Mesh(mesh.devices.reshape(SIZES), AXES)
    placed = (
        P(FSDP, IMG),
        P(IMG),
        P(IMG, FSDP),
        P(),
        P(FSDP, IMG, None),
        P(FSDP, IMG, None),
        P(FSDP, None),
        P(FSDP),
        P(FSDP, None),
        P(),
        P(IMG, FSDP),
    )
    return jax.shard_map(on_device, mesh=fine, in_specs=placed, out_specs=P(IMG, FSDP), check_vma=False)
```

```python
import functools

import jax
import jax.numpy as jnp
from jax import lax
from jax.experimental import pallas as pl
from jax.experimental.pallas import tpu as pltpu
from jax.sharding import Mesh
from jax.sharding import PartitionSpec as P

H = 64
KVH = 8
HD = 128
IMG_BLK = 4
BLOCK_TOK = 128
IMG_TOK = 512
STEPS = 4

NEGATIVE = -1e30
EPSILON = 1e-05

BF16 = jnp.bfloat16
F32 = jnp.float32
MIB = 1 << 20

AXES = ("j", "s", "y", "x", "c")
SIZES = (8, 2, 4, 4, 2)
NEAR = ("s", "y")
IMG = ("x", "c")
FSDP = ("j", "s", "y")

SMEM = pl.BlockSpec(memory_space=pltpu.SMEM)


def cost(flops, size, exps=0):
    return pl.CostEstimate(flops=flops, bytes_accessed=size, transcendentals=exps)


def query_product(core, rows, weights, *sent):
    def kernel(core_ref, rows_ref, weight_ref, *refs):
        *sent_refs, out_ref = refs
        value = rows_ref[...].reshape(256, 1024)
        for pair in (0, 2):
            first, second = weight_ref[2 * pair + core_ref[0]], weight_ref[2 * pair + 2 + core_ref[0]]
            weight = jnp.concatenate([first, second], axis=1)
            total = jnp.dot(value, weight, preferred_element_type=F32).reshape(8, 32, 2 * HD)
            for n in range(2):
                part = total[:, :, n * HD : (n + 1) * HD]
                for sent_ref in sent_refs:
                    part = part + sent_ref[:, pair + n]
                out_ref[:, pair + n] = part

    whole = pl.BlockSpec(memory_space=pltpu.VMEM)
    return pl.pallas_call(
        kernel,
        in_specs=[SMEM, whole, whole] + [whole] * len(sent),
        out_specs=whole,
        out_shape=jax.ShapeDtypeStruct((8, 4, 32, HD), F32),
        compiler_params=pltpu.CompilerParams(vmem_limit_bytes=24 * MIB),
        cost_estimate=cost(256 * 1024 * 1024, 2 * MIB),
    )(core, rows, weights, *sent)


def out_product(core, spot, rows, weights):
    def kernel(core_ref, spot_ref, rows_ref, *refs):
        *weight_refs, own_ref, other_ref = refs
        value = rows_ref[...].reshape(256, 1024)
        for back, weight_ref in enumerate(weight_refs):
            weight = jnp.concatenate([weight_ref[0], weight_ref[1]], axis=1)
            total = jnp.dot(value, weight, preferred_element_type=F32).reshape(4, 2, 32, 2 * HD)
            own = jnp.where(core_ref[0] == 0, total[:, 0], total[:, 1])
            other = jnp.where(core_ref[0] == 0, total[:, 1], total[:, 0])
            place = lax.rem(spot_ref[0] + 4 - back, 4)
            for s in range(2):
                own_ref[place, s] = own[:, :, s * HD : (s + 1) * HD]
                other_ref[place, s] = other[:, :, s * HD : (s + 1) * HD]

    shape = jax.ShapeDtypeStruct((4, 2, 4, 32, HD), F32)
    whole = pl.BlockSpec(memory_space=pltpu.VMEM)
    return pl.pallas_call(
        kernel,
        in_specs=[SMEM, SMEM] + [whole] * 5,
        out_specs=[whole, whole],
        out_shape=(shape, shape),
        compiler_params=pltpu.CompilerParams(vmem_limit_bytes=24 * MIB),
        cost_estimate=cost(2 * 256 * 1024 * 1024, 4 * MIB),
    )(core, spot, rows, *weights)


def attend(slots, marks, parts, gain, caches):
    def kernel(slots_ref, marks_ref, part_ref, gain_ref, cache_ref, out_ref, score_ref, expo_ref):
        low = lax.broadcasted_iota(jnp.int32, (8, HD), 0) < 4
        places = []
        for s in range(8):
            slot = [jnp.clip(slots_ref[s, k], 0, 15) for k in range(2)]
            places.append([(one // 2, one % 2) for one in slot])
        heads = []
        for h in range(8):
            value = jnp.sum(part_ref[h % 4 * 2 + h // 4], axis=0)
            inverse = lax.rsqrt(jnp.mean(value * value, axis=-1, keepdims=True) + EPSILON)
            heads.append(value * inverse * gain_ref[...])
        for s in range(8):
            tiles = []
            for h in range(0, 8, 2):
                even, odd = (head[s // 2 * 8 : s // 2 * 8 + 8] for head in heads[h : h + 2])
                if s % 2 == 0:
                    tiles.append(jnp.where(low, even, pltpu.roll(odd, 4, 0)))
                else:
                    tiles.append(jnp.where(low, pltpu.roll(even, 4, 0), odd))
            rows = jnp.concatenate(tiles, axis=0).astype(BF16)
            for k in range(2):
                score_ref[s, :, k * IMG_TOK : (k + 1) * IMG_TOK] = lax.dot_general(
                    rows,
                    cache_ref[places[s][k][0], 0, places[s][k][1]],
                    (((1,), (1,)), ((), ())),
                    preferred_element_type=F32,
                )
        totals = []
        for s in range(8):
            blocks = [
                jnp.broadcast_to(marks_ref[8 * s : 8 * s + 8, b : b + 1], (8, BLOCK_TOK)) for b in range(2 * IMG_BLK)
            ]
            visible = (jnp.concatenate(blocks, axis=1) > 0.5).reshape(1, 8, 2 * IMG_TOK)
            score = (score_ref[s] * HD ** (-0.5)).reshape(4, 8, 2 * IMG_TOK)
            peak = jnp.max(jnp.where(visible, score, NEGATIVE), axis=-1, keepdims=True)
            expo = jnp.where(visible, jnp.exp(score - peak), 0.0)
            totals.append(jnp.sum(expo, axis=-1, keepdims=True))
            expo_ref[s] = expo.reshape(32, 2 * IMG_TOK).astype(BF16)
        results = []
        for s in range(8):
            first, second = (cache_ref[place[0], 1, place[1]] for place in places[s])
            weighted = jnp.dot(expo_ref[s, :, :IMG_TOK], first, preferred_element_type=F32)
            weighted += jnp.dot(expo_ref[s, :, IMG_TOK:], second, preferred_element_type=F32)
            results.append(weighted.reshape(4, 8, HD) / totals[s])
        for h in range(8):
            tiles = []
            for pair in range(4):
                even, odd = results[2 * pair][h // 2], results[2 * pair + 1][h // 2]
                if h % 2 == 0:
                    tiles.append(jnp.where(low, even, pltpu.roll(odd, 4, 0)))
                else:
                    tiles.append(jnp.where(low, pltpu.roll(even, 4, 0), odd))
            tile = jnp.concatenate(tiles, axis=0).astype(BF16)
            out_ref[:, h * HD : (h + 1) * HD] = tile

    whole = pl.BlockSpec(memory_space=pltpu.VMEM)
    return pl.pallas_call(
        kernel,
        in_specs=[SMEM, whole, whole, whole, whole],
        out_specs=whole,
        out_shape=jax.ShapeDtypeStruct((32, KVH * HD), BF16),
        scratch_shapes=[pltpu.VMEM((8, 32, 2 * IMG_TOK), F32), pltpu.VMEM((8, 32, 2 * IMG_TOK), BF16)],
        compiler_params=pltpu.CompilerParams(vmem_limit_bytes=24 * MIB),
        cost_estimate=cost(4 * 2 * 32 * 8 * 512 * 128, 5 * MIB, 2 * 8 * 32 * 512),
    )(slots, marks, parts, gain, caches)


def on_device(
    tokens,
    norm_gain,
    w_query,
    query_gain,
    key_cache,
    value_cache,
    block_mask,
    image_counts,
    image_slot,
    attn_gate,
    w_out,
):
    query_weights = lax.all_gather(w_query, "j")
    caches = jnp.stack([key_cache[0], value_cache[0]]).reshape(2, 1024, KVH, HD).transpose(2, 0, 1, 3)
    caches, tokens = lax.optimization_barrier((caches, tokens))
    caches = lax.all_to_all(caches, IMG, 0, 0, tiled=True)
    scaled = (tokens.astype(F32) * norm_gain).astype(BF16)
    scaled = lax.all_gather(lax.all_gather(scaled, "s"), "y")
    out_weights = [lax.all_gather(w_out, "s")]
    for ahead in range(1, 4):
        out_weights.append(lax.ppermute(out_weights[0], "y", [(a, (a + ahead) % 4) for a in range(4)]))
    live = jnp.arange(2, dtype=jnp.int32)[None, :] < image_counts[:, None]
    marks = (block_mask.reshape(8, STEPS, 2, IMG_BLK) == 1) & live[:, None, :, None]
    marks = jnp.tile(marks.reshape(8, STEPS, 2 * IMG_BLK).astype(F32), (1, 2, 1)).reshape(64, 2 * IMG_BLK)
    scaled, out_weights, marks = lax.optimization_barrier((scaled, out_weights, marks))

    core = lax.axis_index("c").reshape(1)
    swap = [(0, 1), (1, 0)]
    scaled = scaled.reshape(8, 32, 1024)
    other = query_product(1 - core, scaled, query_weights)
    parts = query_product(core, scaled, query_weights, lax.ppermute(other, "c", swap)).reshape(32, 32, HD)
    parts, caches = lax.optimization_barrier((parts, caches))
    parts = lax.all_to_all(parts, ("y", "s", "x"), 0, 0, tiled=True).reshape(8, 4, 32, HD)
    caches = caches.reshape(8, 2, 2, IMG_TOK, HD)
    attended = attend(image_slot, marks, parts, query_gain.reshape(1, HD), caches)

    spot = lax.axis_index("y").reshape(1)
    own, other = out_product(core, spot, lax.all_gather(attended, "j"), out_weights)
    partial = (own + lax.ppermute(other, "c", swap)).astype(BF16).reshape(32, 32, HD)
    partial = lax.all_to_all(partial, ("y", "s", "x"), 0, 0, tiled=True).reshape(4, 2, 4, 32, HD)
    mixed = (jnp.tanh(attn_gate[0]) * jnp.sum(partial.astype(F32), axis=2)).astype(BF16)
    return mixed.swapaxes(0, 1).reshape(256, HD)


def solution(mesh):
    fine = Mesh(mesh.devices.reshape(SIZES), AXES)
    placed = (
        P(FSDP, IMG),
        P(IMG),
        P(IMG, FSDP),
        P(),
        P(FSDP, IMG, None),
        P(FSDP, IMG, None),
        P(FSDP, None),
        P(FSDP),
        P(FSDP, None),
        P(),
        P(IMG, FSDP),
    )
    return jax.shard_map(on_device, mesh=fine, in_specs=placed, out_specs=P(IMG, FSDP), check_vma=False)
```
